32 devices in a mesh: rep: 2 (over y), dp: 4 (over z), mp: 2 (over x), sub: 2 (over core).
Axes of the slice: x: 2, y: 2, z: 4, core: 2. Of those that a mesh axis runs over, the one named last changes fastest.
Arguments:
- activations: bfloat16 [2048, 2048], P(('rep', 'dp')), parts along dimension 0, may hold values from -6 to 6
- cotangent: bfloat16 [2048, 2, 512], P(('rep', 'dp'), 'mp', 'sub'), parts along dimension 0, may hold values from -6 to 6
- owner_table: int32 [4, 4], P(('rep', 'mp')), parts along dimension 0, may hold values from 0 to 3, each once within a row
Outputs:
- update: bfloat16 [16, 512, 512], P(('rep', 'mp'), 'dp', 'sub'), parts along dimension 0
The draws below stay inside these ranges and needn't reach their ends.
There are 2 independent parts, one for each index of `rep`. The reference program is written for one: setup_inputs(seed, part) draws one part's arguments, and reference() takes and returns one part's arrays. A program takes and returns all parts, laid end to end along the dimension named above; each array names one. Nothing has to cross between parts.
Inputs may be any that keep to these rules, and one draw needn't show every extreme that they name: Each row of owner_table names every block number of its layer group exactly once.
All inputs are finite; a program needn't handle non-finite values.
Results may differ from the reference program's by a relative error of at most 0.015.
Values may be sent and summed in bfloat16 or wider, within the bound.
A program may use at most 64 MiB of HBM per device.

```python
import math
import jax
import jax.numpy as jnp
from jax import lax

D = 2048
B = 512
RB = 4
CB = 1
TOK_DEV = 256
TOKENS = 1024
ITERS = 2
N_DP = 4
N_MP = 2


def shard_levels(rng, extent, split, low, high):
    def one(axis_at, shards_of):
        steps = jax.random.uniform(jax.random.fold_in(jax.random.fold_in(rng, 6), axis_at), (shards_of,), jnp.float32, low / len(split), high / len(split))
        return jnp.repeat(jnp.exp(steps), extent[axis_at] // shards_of).reshape((-1,) + (1,) * (len(extent) - axis_at - 1))

    gain = one(*split[0])
    for cut in split[1:]:
        gain = gain * one(*cut)
    return gain


def normal_values(stream_key, extent, scale, limit, cuts=(), kind=jnp.bfloat16):
    drawn = jax.random.normal(stream_key, extent, jnp.float32) * scale
    if len(cuts) > 0:
        drawn = shard_levels(stream_key, extent, cuts, -0.22, 0.18) * drawn
    return jnp.clip(drawn, min=-limit, max=limit).astype(kind)


def setup_inputs(seed: int = 0, part: int = 0) -> dict:
    seeds = jax.random.split(jax.random.key(seed), 4)
    own_keys = jax.random.split(jax.random.fold_in(seeds[3], part), 4)
    activations = normal_values(own_keys[0], (TOKENS, D), 1.0, 6.0, ((0, 4),))
    cotangent = normal_values(own_keys[1], (TOKENS, N_MP * CB, B), 1.0, 6.0, ((0, 4), (1, 2), (2, 2)))
    owner_table = jax.vmap(lambda own: jax.random.permutation(own, N_DP))(jax.random.split(own_keys[2], N_MP)).reshape((N_MP, N_DP)).astype(jnp.int32)
    return {"activations": activations, "cotangent": cotangent, "owner_table": owner_table}


damping_rel = 0.05

def matmul_high(left_mat, right_mat):
    return jnp.dot(left_mat, right_mat, precision=lax.Precision.HIGHEST)

def newton_root(statistic):
    identity = jnp.eye(statistic.shape[0], dtype=statistic.dtype)
    damped = statistic + damping_rel * (jnp.trace(statistic) / statistic.shape[0]) * identity
    frob = jnp.sqrt(jnp.sum(damped * damped))
    scale_init = 2.5 / frob
    root_now = scale_init ** 0.25 * identity
    coupled = scale_init * damped
    for sweep in range(ITERS):
        factor = (5.0 * identity - coupled) * 0.25
        root_now = matmul_high(root_now, factor)
        squared = matmul_high(factor, factor)
        fourth = matmul_high(squared, squared)
        coupled = matmul_high(fourth, coupled)
    return root_now

def precondition_block(gradient):
    left_root = newton_root(matmul_high(gradient, gradient.T))
    right_root = newton_root(matmul_high(gradient.T, gradient))
    left_b = left_root.astype(jnp.bfloat16)
    right_b = right_root.astype(jnp.bfloat16)
    grad_b = gradient.astype(jnp.bfloat16)
    carried = jnp.dot(grad_b, right_b, preferred_element_type=jnp.float32).astype(jnp.bfloat16)
    product = jnp.dot(left_b, carried, preferred_element_type=jnp.float32)
    return (product * math.sqrt(B)).astype(jnp.bfloat16)

def reference(activations, cotangent, owner_table):
    width = N_MP * CB * B
    act_shards = activations.reshape(N_DP, TOK_DEV, D)
    cot_shards = cotangent.reshape(N_DP, TOK_DEV, width)

    def accumulate(running, shard_pair):
        act_piece, cot_piece = shard_pair
        partial_value = jnp.dot(act_piece.T, cot_piece, preferred_element_type=jnp.float32).astype(jnp.bfloat16)
        partial_value = lax.optimization_barrier(partial_value)
        return (running + partial_value.astype(jnp.float32), None)
    gradient, unused = lax.scan(accumulate, jnp.zeros((D, width), jnp.float32), (act_shards, cot_shards))
    blocks = gradient.reshape(RB, B, N_MP, CB, B).transpose(2, 0, 3, 1, 4).reshape(N_MP * N_DP, B, B)
    offsets = (jnp.arange(N_MP, dtype=jnp.int32) * N_DP)[:, None]
    chosen = (offsets + owner_table.astype(jnp.int32)).reshape(-1)
    owned = jnp.take(blocks, chosen, axis=0)
    return lax.map(precondition_block, owned)
```

```python
import functools
import math

import jax
import jax.numpy as jnp
from jax import lax
from jax.experimental import pallas as pl
from jax.experimental.pallas import tpu as pltpu
from jax.sharding import PartitionSpec as P

B = 512
CHUNKS = 2
DAMPING = 0.05
MESH = pl.DeviceIdType.MESH
F32 = jnp.float32
BF16 = jnp.bfloat16


def kernel(
    dp, col_count, table, act_hbm, cot_hbm, out,
    act, cot, to_right, to_left, from_left, from_right, grad, own, peer, kmat, carried, update,
    load_sem, right_send, left_send, left_recv, right_recv, sub_send, sub_recv, out_send, out_recv,
):
    z = lax.axis_index("dp")
    s = lax.axis_index("sub")
    half = own.shape[1]
    rows = B // CHUNKS
    total = dp * CHUNKS
    out_rows = B // dp

    pieces = act.shape[0]
    loads = [pltpu.make_async_copy(cot_hbm, cot, load_sem.at[pieces])]
    for i in range(pieces):
        loads.append(pltpu.make_async_copy(act_hbm.at[:, pl.ds(i * rows, rows)], act.at[i], load_sem.at[i]))
    for load in loads:
        load.start()
    barrier = pltpu.get_barrier_semaphore()
    for k in range(1, dp):
        pl.semaphore_signal(barrier, inc=1, device_id={"dp": lax.rem(z + k, dp)}, device_id_type=MESH)
    pl.semaphore_signal(barrier, inc=1, device_id={"sub": 1 - s}, device_id_type=MESH)
    for load in loads:
        load.wait()
    pl.semaphore_wait(barrier, dp)

    def partial(owner, part):
        block = table[0, owner]
        return lax.dot_general(
            act[lax.div(block, col_count) * CHUNKS + part], cot[lax.rem(block, col_count)],
            (((0,), (0,)), ((), ())), preferred_element_type=F32,
        )

    def rightward(n):
        return pltpu.make_async_remote_copy(
            src_ref=to_right.at[n], dst_ref=from_left.at[n],
            send_sem=right_send.at[n], recv_sem=left_recv.at[n],
            device_id={"dp": lax.rem(z + 1, dp)}, device_id_type=MESH,
        )

    def leftward(n):
        return pltpu.make_async_remote_copy(
            src_ref=to_left.at[n], dst_ref=from_right.at[n],
            send_sem=left_send.at[n], recv_sem=right_recv.at[n],
            device_id={"dp": lax.rem(z + dp - 1, dp)}, device_id_type=MESH,
        )

    def tick(t, carry):
        n = t - z
        owner = dp - 1 - n // CHUNKS

        @pl.when((n >= 0) & (n < total) & (owner > z))
        def _():
            piece = partial(owner, n % CHUNKS)

            @pl.when(z == 0)
            def _():
                to_right[n] = piece.astype(BF16)

            @pl.when(z > 0)
            def _():
                rightward(n).wait_recv()
                to_right[n] = (piece + from_left[n].astype(F32)).astype(BF16)

            rightward(n).start()

        m = t - (dp - 1 - z)
        owner_l = m // CHUNKS

        @pl.when((m >= 0) & (m < total) & (owner_l < z))
        def _():
            piece = partial(owner_l, m % CHUNKS)

            @pl.when(z == dp - 1)
            def _():
                to_left[m] = piece.astype(BF16)

            @pl.when(z < dp - 1)
            def _():
                leftward(m).wait_recv()
                to_left[m] = (piece + from_right[m].astype(F32)).astype(BF16)

            leftward(m).start()

        return carry

    lax.fori_loop(0, total + dp - 1, tick, 0)

    def exchange(part):
        return pltpu.make_async_remote_copy(
            src_ref=own.at[pl.ds(part * rows, rows)], dst_ref=peer.at[pl.ds(part * rows, rows)],
            send_sem=sub_send.at[part], recv_sem=sub_recv.at[part],
            device_id={"sub": 1 - s}, device_id_type=MESH,
        )

    for part in range(CHUNKS):
        here = pl.ds(part * rows, rows)
        grad[here, :] = partial(z, part)

        @pl.when(z > 0)
        def _():
            n = (dp - 1 - z) * CHUNKS + part
            rightward(n).wait_recv()
            grad[here, :] += from_left[n].astype(F32)

        @pl.when(z < dp - 1)
        def _():
            n = z * CHUNKS + part
            leftward(n).wait_recv()
            grad[here, :] += from_right[n].astype(F32)

        own[here, :] = grad[here, :].astype(BF16)
        exchange(part).start()

    nt = (((1,), (1,)), ((), ()))
    mine = own[...]
    stat = lax.dot_general(mine, mine, nt, preferred_element_type=F32)
    for part in range(CHUNKS):
        exchange(part).wait()
    theirs = peer[...]
    stat = stat + lax.dot_general(theirs, theirs, nt, preferred_element_type=F32)
    diagonal = lax.broadcasted_iota(jnp.int32, (B, B), 0) == lax.broadcasted_iota(jnp.int32, (B, B), 1)

    def total_of(x):
        return jnp.sum(jnp.sum(x, axis=0, keepdims=True), axis=1, keepdims=True)

    trace = total_of(jnp.where(diagonal, stat, 0.0))
    shift = DAMPING / B * trace
    damped = stat + jnp.where(diagonal, shift, 0.0)
    z_scale = 2.5 / jnp.sqrt(total_of(damped * damped))
    x = z_scale * damped
    xb = x.astype(BF16)
    x2 = jnp.dot(xb, xb, preferred_element_type=F32)
    d2 = 0.0625 * (10.0 * x - x2)
    fx = 0.25 * (5.0 * x - x2)
    d2b = d2.astype(BF16)
    d4 = 3.125 * d2 - jnp.dot(d2b, d2b, preferred_element_type=F32)
    w = jnp.dot(d4.astype(BF16), fx.astype(BF16), preferred_element_type=F32)
    kmat[...] = (0.3125 * x + 0.6103515625 * fx - 0.25 * w).astype(BF16)
    carried[...] = 1.5625 * grad[...] - jnp.dot(kmat[...], mine, preferred_element_type=F32)
    carried_b = carried[...].astype(BF16)
    gain = math.sqrt(B) * jnp.sqrt(z_scale)

    def deliver(k):
        there = lax.rem(z + k, dp)
        return pltpu.make_async_remote_copy(
            src_ref=update.at[there], dst_ref=out.at[z],
            send_sem=out_send.at[k - 1], recv_sem=out_recv.at[k - 1],
            device_id={"dp": there}, device_id_type=MESH,
        )

    def update_rows(there):
        at = pl.ds(pl.multiple_of(there * out_rows, out_rows), out_rows)
        product = jnp.dot(kmat[at, :], carried_b, preferred_element_type=F32)
        return (gain * (1.5625 * carried[at, :] - product)).astype(BF16)

    for k in range(1, dp):
        there = lax.rem(z + k, dp)
        update[there] = update_rows(there)
        deliver(k).start()
    out[z] = update_rows(z)

    for n in range(total):
        @pl.when(dp - 1 - n // CHUNKS > z)
        def _():
            rightward(n).wait_send()

        @pl.when(n // CHUNKS < z)
        def _():
            leftward(n).wait_send()
    for k in range(1, dp):
        came = lax.rem(z + dp - k, dp)
        deliver(k).wait_send()
        pltpu.make_async_remote_copy(
            src_ref=update.at[came], dst_ref=out.at[came],
            send_sem=out_send.at[k - 1], recv_sem=out_recv.at[k - 1],
            device_id={"dp": came}, device_id_type=MESH,
        ).wait_recv()


def shards(dp, activations, cotangent, owner_table):
    tokens, width = activations.shape
    col_count, half = cotangent.shape[1:]
    cot = cotangent.transpose(1, 0, 2)
    rows = B // CHUNKS
    total = dp * CHUNKS
    hbm = pl.BlockSpec(memory_space=pltpu.HBM)
    dma = pltpu.SemaphoreType.DMA
    return pl.pallas_call(
        functools.partial(kernel, dp, col_count),
        out_shape=jax.ShapeDtypeStruct((dp, B // dp, half), BF16),
        in_specs=[pl.BlockSpec(memory_space=pltpu.SMEM), hbm, hbm],
        out_specs=pl.BlockSpec(memory_space=pltpu.VMEM),
        scratch_shapes=[
            pltpu.VMEM((width // rows, tokens, rows), BF16),
            pltpu.VMEM((col_count, tokens, half), BF16),
            pltpu.VMEM((total, rows, half), BF16),
            pltpu.VMEM((total, rows, half), BF16),
            pltpu.VMEM((total, rows, half), BF16),
            pltpu.VMEM((total, rows, half), BF16),
            pltpu.VMEM((B, half), F32),
            pltpu.VMEM((B, half), BF16),
            pltpu.VMEM((B, half), BF16),
            pltpu.VMEM((B, B), BF16),
            pltpu.VMEM((B, half), F32),
            pltpu.VMEM((dp, B // dp, half), BF16),
            dma((width // rows + 1,)), dma((total,)), dma((total,)), dma((total,)), dma((total,)),
            dma((CHUNKS,)), dma((CHUNKS,)), dma((dp - 1,)), dma((dp - 1,)),
        ],
        compiler_params=pltpu.CompilerParams(
            collective_id=0, has_side_effects=True, vmem_limit_bytes=48 * 1024 * 1024
        ),
    )(owner_table, activations, cot)


def solution(mesh):
    in_specs = (P(("rep", "dp"), None), P(("rep", "dp"), "mp", "sub"), P(("rep", "mp"), None))
    out_specs = P(("rep", "mp"), "dp", "sub")
    return jax.shard_map(
        functools.partial(shards, mesh.shape["dp"]),
        mesh=mesh, in_specs=in_specs, out_specs=out_specs, check_vma=False,
    )
```

```python
import functools
import math

import jax
import jax.numpy as jnp
from jax import lax
from jax.experimental import pallas as pl
from jax.experimental.pallas import tpu as pltpu
from jax.sharding import PartitionSpec as P

B = 512
PIECES = 2
DAMPING = 0.05
MESH = pl.DeviceIdType.MESH
F32 = jnp.float32
BF16 = jnp.bfloat16


def kernel(
    dp, mp, col_count, table, act_hbm, cot_hbm, out,
    act, cot, act_in, both, grad, kmat, carried, update, landed,
    load_sem, act_send, act_recv, share_send, share_recv, cot_send, cot_recv, pair_send, pair_recv,
    swap_send, swap_recv, out_send, out_recv,
):
    z = lax.axis_index("dp")
    m = lax.axis_index("mp")
    s = lax.axis_index("sub")
    half = B // 2
    tokens = act.shape[0]
    part = tokens // mp
    mine_rows = pl.ds(pl.multiple_of(m * part, part), part)
    block_col = lax.rem(z, col_count)
    out_rows = B // dp

    def remote(src, dst, send, recv, where):
        return pltpu.make_async_remote_copy(
            src_ref=src, dst_ref=dst, send_sem=send, recv_sem=recv, device_id=where, device_id_type=MESH,
        )

    def columns(owner):
        return pl.ds(pl.multiple_of((lax.div(owner, col_count) * 2 + s) * half, half), half)

    load_act = pltpu.make_async_copy(act_hbm.at[:, columns(z)], act, load_sem.at[0])
    load_cot = pltpu.make_async_copy(cot_hbm, cot.at[z, s], load_sem.at[1])
    load_act.start()
    load_cot.start()
    barrier = pltpu.get_barrier_semaphore()
    for k in range(1, dp):
        pl.semaphore_signal(barrier, inc=1, device_id={"dp": lax.rem(z + k, dp)}, device_id_type=MESH)
    for k in range(1, mp):
        pl.semaphore_signal(barrier, inc=1, device_id={"mp": lax.rem(m + k, mp)}, device_id_type=MESH)
    pl.semaphore_signal(barrier, inc=1, device_id={"sub": 1 - s}, device_id_type=MESH)
    pl.semaphore_wait(barrier, dp + mp - 1)

    def pass_on(side, src, d, q):
        there = z + 1 if side == 0 else z - 1
        at = pl.ds(q * (tokens // PIECES), tokens // PIECES)
        return remote(
            src.at[:, at], cot.at[d, s, :, at], cot_send.at[side, d, q], cot_recv.at[d, q], {"dp": there}
        )

    def to_pair(src, d):
        return remote(src, cot.at[d, s, block_col], pair_send.at[d], pair_recv.at[d], {"sub": 1 - s})

    def pair_came(d):
        return remote(
            cot.at[d, 1 - s, block_col], cot.at[d, 1 - s, block_col], pair_send.at[d], pair_recv.at[d],
            {"sub": 1 - s},
        )

    def send_act(owner):
        return remote(
            act_hbm.at[mine_rows, columns(owner)], act_in.at[z, m],
            act_send.at[owner], act_recv.at[z], {"dp": owner},
        )

    def act_came(d):
        return remote(act_in.at[d, m], act_in.at[d, m], act_send.at[d], act_recv.at[d], {"dp": d})

    def share(d, k):
        there = lax.rem(m + k, mp)
        return remote(
            act_in.at[d, m], act_in.at[d, m], share_send.at[d, k - 1], share_recv.at[d, k - 1], {"mp": there},
        )

    def share_came(d, k):
        came = lax.rem(m + mp - k, mp)
        return remote(
            act_in.at[d, came], act_in.at[d, came], share_send.at[d, k - 1], share_recv.at[d, k - 1],
            {"mp": came},
        )

    has_next = (z < dp - 1, z > 0)

    def each(k, body):
        for side in range(2):
            d = z - k if side == 0 else z + k

            @pl.when((d >= 0) & (d < dp))
            def _():
                body(side, d)

    for side in range(2):
        @pl.when(has_next[side])
        def _():
            for q in range(PIECES):
                pass_on(side, cot_hbm, z, q).start()
    to_pair(cot_hbm.at[block_col], z).start()
    for k in range(1, dp):
        each(k, lambda side, d: send_act(d).start())

    def add(lhs, d, first):
        for h in range(2):
            piece = lax.dot_general(
                lhs, cot[d, h, block_col], (((0,), (0,)), ((), ())), preferred_element_type=F32
            )
            if first:
                grad[h] = piece
            else:
                grad[h] += piece

    load_act.wait()
    load_cot.wait()
    pair_came(z).wait_recv()
    add(act[...], z, True)

    def cot_arrival(side, d):
        for q in range(PIECES):
            pass_on(side, cot.at[d, s], d, q).wait_recv()

            @pl.when(has_next[side])
            def _():
                pass_on(side, cot.at[d, s], d, q).start()

        to_pair(cot.at[d, s, block_col], d).start()

    def act_arrival(side, d):
        act_came(d).wait_recv()
        for k in range(1, mp):
            share(d, k).start()

    def accumulate(side, d):
        for k in range(1, mp):
            share_came(d, k).wait_recv()
        pair_came(d).wait_recv()
        add(act_in[d].reshape(tokens, half), d, False)

    each(1, cot_arrival)
    each(1, act_arrival)
    for k in range(2, dp):
        each(k, act_arrival)
        each(k, cot_arrival)
        each(k - 1, accumulate)
    each(dp - 1, accumulate)

    for h in range(2):
        both[s, :, pl.ds(h * half, half)] = grad[h].astype(BF16)
    swap = remote(both.at[s], both.at[s], swap_send, swap_recv, {"sub": 1 - s})
    swap.start()
    swap.wait_send()
    remote(both.at[1 - s], both.at[1 - s], swap_send, swap_recv, {"sub": 1 - s}).wait_recv()

    nt = (((1,), (1,)), ((), ()))
    whole = both[...].reshape(B, B)
    stat = lax.dot_general(whole, whole, nt, preferred_element_type=F32)
    mine = both[:, :, pl.ds(pl.multiple_of(s * half, half), half)].reshape(B, half)
    diagonal = lax.broadcasted_iota(jnp.int32, (B, B), 0) == lax.broadcasted_iota(jnp.int32, (B, B), 1)

    def total_of(x):
        return jnp.sum(jnp.sum(x, axis=0, keepdims=True), axis=1, keepdims=True)

    trace = total_of(jnp.where(diagonal, stat, 0.0))
    shift = DAMPING / B * trace
    damped = stat + jnp.where(diagonal, shift, 0.0)
    z_scale = 2.5 / jnp.sqrt(total_of(damped * damped))
    x = z_scale * damped
    xb = x.astype(BF16)
    x2 = jnp.dot(xb, xb, preferred_element_type=F32)
    d2 = 0.0625 * (10.0 * x - x2)
    fx = 0.25 * (5.0 * x - x2)
    d2b = d2.astype(BF16)
    d4 = 3.125 * d2 - jnp.dot(d2b, d2b, preferred_element_type=F32)
    w = jnp.dot(d4.astype(BF16), fx.astype(BF16), preferred_element_type=F32)
    kmat[...] = (0.3125 * x + 0.6103515625 * fx - 0.25 * w).astype(BF16)
    carried[...] = 1.5625 * mine.astype(F32) - jnp.dot(kmat[...], mine, preferred_element_type=F32)
    carried_b = carried[...].astype(BF16)
    gain = math.sqrt(B) * jnp.sqrt(z_scale)

    def deliver(k):
        there = lax.rem(z + k, dp)
        return remote(
            update.at[there], landed.at[z], out_send.at[k - 1], out_recv.at[k - 1], {"dp": there}
        )

    def delivered(k):
        came = lax.rem(z + dp - k, dp)
        return remote(
            update.at[came], landed.at[came], out_send.at[k - 1], out_recv.at[k - 1], {"dp": came}
        )

    def update_rows(there):
        at = pl.ds(pl.multiple_of(there * out_rows, out_rows), out_rows)
        product = jnp.dot(kmat[at, :], carried_b, preferred_element_type=F32)
        return (gain * (1.5625 * carried[at, :] - product)).astype(BF16)

    for k in range(1, dp):
        there = lax.rem(z + k, dp)
        update[there] = update_rows(there)
        deliver(k).start()
    landed[z] = update_rows(z)

    def sent(side, d):
        send_act(d).wait_send()
        to_pair(cot.at[d, s, block_col], d).wait_send()
        for k in range(1, mp):
            share(d, k).wait_send()

        @pl.when(has_next[side])
        def _():
            for q in range(PIECES):
                pass_on(side, cot.at[d, s], d, q).wait_send()

    to_pair(cot_hbm.at[block_col], z).wait_send()
    for side in range(2):
        @pl.when(has_next[side])
        def _():
            for q in range(PIECES):
                pass_on(side, cot_hbm, z, q).wait_send()
    for k in range(1, dp):
        each(k, sent)
    for k in range(1, dp):
        deliver(k).wait_send()
        delivered(k).wait_recv()
    for slot in range(dp):
        out[slot] = landed[table[0, slot]]


def shards(dp, mp, activations, cotangent, owner_table):
    tokens = activations.shape[0]
    col_count, half = cotangent.shape[1:]
    cot = cotangent.transpose(1, 0, 2)
    hbm = pl.BlockSpec(memory_space=pltpu.HBM)
    dma = pltpu.SemaphoreType.DMA
    return pl.pallas_call(
        functools.partial(kernel, dp, mp, col_count),
        out_shape=jax.ShapeDtypeStruct((dp, B // dp, half), BF16),
        in_specs=[pl.BlockSpec(memory_space=pltpu.SMEM), hbm, hbm],
        out_specs=pl.BlockSpec(memory_space=pltpu.VMEM),
        scratch_shapes=[
            pltpu.VMEM((tokens, half), BF16),
            pltpu.VMEM((dp, 2, col_count, tokens, half), BF16),
            pltpu.VMEM((dp, mp, tokens // mp, half), BF16),
            pltpu.VMEM((2, half, B), BF16),
            pltpu.VMEM((2, half, half), F32),
            pltpu.VMEM((B, B), BF16),
            pltpu.VMEM((B, half), F32),
            pltpu.VMEM((dp, B // dp, half), BF16),
            pltpu.VMEM((dp, B // dp, half), BF16),
            dma((2,)), dma((dp,)), dma((dp,)), dma((dp, mp - 1)), dma((dp, mp - 1)), dma((2, dp, PIECES)), dma((dp, PIECES)),
            dma((dp,)), dma((dp,)), dma, dma, dma((dp - 1,)), dma((dp - 1,)),
        ],
        compiler_params=pltpu.CompilerParams(
            collective_id=0, has_side_effects=True, vmem_limit_bytes=60 * 1024 * 1024
        ),
    )(owner_table, activations, cot)


def solution(mesh):
    in_specs = (P(("rep", "dp"), None), P(("rep", "dp"), "mp", "sub"), P(("rep", "mp"), None))
    out_specs = P(("rep", "mp"), "dp", "sub")
    return jax.shard_map(
        functools.partial(shards, mesh.shape["dp"], mesh.shape["mp"]),
        mesh=mesh, in_specs=in_specs, out_specs=out_specs, check_vma=False,
    )
```

```python
import functools
import math

import jax
import jax.numpy as jnp
from jax import lax
from jax.experimental import pallas as pl
from jax.experimental.pallas import tpu as pltpu
from jax.sharding import PartitionSpec as P

B = 512
PIECES = 2
DAMPING = 0.05
MESH = pl.DeviceIdType.MESH
F32 = jnp.float32
BF16 = jnp.bfloat16


def kernel(
    dp, mp, col_count, table, act_hbm, cot_hbm, out,
    act, cot, act_in, both, grad, kmat, carried, update, landed,
    load_sem, act_send, act_recv, share_send, share_recv, cot_send, cot_recv, pair_send, pair_recv,
    swap_send, swap_recv, out_send, out_recv,
):
    z = lax.axis_index("dp")
    m = lax.axis_index("mp")
    s = lax.axis_index("sub")
    half = B // 2
    tokens = act.shape[0]
    part = tokens // mp
    mine_rows = pl.ds(pl.multiple_of(m * part, part), part)
    block_col = lax.rem(z, col_count)
    out_rows = B // dp

    def remote(src, dst, send, recv, where):
        return pltpu.make_async_remote_copy(
            src_ref=src, dst_ref=dst, send_sem=send, recv_sem=recv, device_id=where, device_id_type=MESH,
        )

    def columns(owner):
        return pl.ds(pl.multiple_of((lax.div(owner, col_count) * 2 + s) * half, half), half)

    load_act = pltpu.make_async_copy(act_hbm.at[:, columns(z)], act, load_sem.at[0])
    load_cot = pltpu.make_async_copy(cot_hbm, cot.at[z, s], load_sem.at[1])
    load_act.start()
    load_cot.start()
    barrier = pltpu.get_barrier_semaphore()
    for k in range(1, dp):
        pl.semaphore_signal(barrier, inc=1, device_id={"dp": lax.rem(z + k, dp)}, device_id_type=MESH)
    for k in range(1, mp):
        pl.semaphore_signal(barrier, inc=1, device_id={"mp": lax.rem(m + k, mp)}, device_id_type=MESH)
    pl.semaphore_signal(barrier, inc=1, device_id={"sub": 1 - s}, device_id_type=MESH)
    pl.semaphore_wait(barrier, dp + mp - 1)

    def pass_on(side, src, d, q):
        there = z + 1 if side == 0 else z - 1
        at = pl.ds(q * (tokens // PIECES), tokens // PIECES)
        return remote(
            src.at[:, at], cot.at[d, s, :, at], cot_send.at[side, d, q], cot_recv.at[d, q], {"dp": there}
        )

    def to_pair(src, d):
        return remote(src, cot.at[d, s, block_col], pair_send.at[d], pair_recv.at[d], {"sub": 1 - s})

    def pair_came(d):
        return remote(
            cot.at[d, 1 - s, block_col], cot.at[d, 1 - s, block_col], pair_send.at[d], pair_recv.at[d],
            {"sub": 1 - s},
        )

    def send_act(owner):
        return remote(
            act_hbm.at[mine_rows, columns(owner)], act_in.at[z, m],
            act_send.at[owner], act_recv.at[z], {"dp": owner},
        )

    def act_came(d):
        return remote(act_in.at[d, m], act_in.at[d, m], act_send.at[d], act_recv.at[d], {"dp": d})

    def share(d, k):
        there = lax.rem(m + k, mp)
        return remote(
            act_in.at[d, m], act_in.at[d, m], share_send.at[d, k - 1], share_recv.at[d, k - 1], {"mp": there},
        )

    def share_came(d, k):
        came = lax.rem(m + mp - k, mp)
        return remote(
            act_in.at[d, came], act_in.at[d, came], share_send.at[d, k - 1], share_recv.at[d, k - 1],
            {"mp": came},
        )

    has_next = (z < dp - 1, z > 0)

    def each(k, body):
        for side in range(2):
            d = z - k if side == 0 else z + k

            @pl.when((d >= 0) & (d < dp))
            def _():
                body(side, d)

    for side in range(2):
        @pl.when(has_next[side])
        def _():
            for q in range(PIECES):
                pass_on(side, cot_hbm, z, q).start()
    to_pair(cot_hbm.at[block_col], z).start()
    for k in range(1, dp):
        each(k, lambda side, d: send_act(d).start())

    def add(lhs, d, first):
        for h in range(2):
            piece = lax.dot_general(
                lhs, cot[d, h, block_col], (((0,), (0,)), ((), ())), preferred_element_type=F32
            )
            if first:
                grad[h] = piece
            else:
                grad[h] += piece

    load_act.wait()
    load_cot.wait()
    pair_came(z).wait_recv()
    add(act[...], z, True)

    def cot_arrival(side, d):
        for q in range(PIECES):
            pass_on(side, cot.at[d, s], d, q).wait_recv()

            @pl.when(has_next[side])
            def _():
                pass_on(side, cot.at[d, s], d, q).start()

        to_pair(cot.at[d, s, block_col], d).start()

    def act_arrival(side, d):
        act_came(d).wait_recv()
        for k in range(1, mp):
            share(d, k).start()

    def accumulate(side, d):
        for k in range(1, mp):
            share_came(d, k).wait_recv()
        pair_came(d).wait_recv()
        add(act_in[d].reshape(tokens, half), d, False)

    each(1, cot_arrival)
    each(1, act_arrival)
    for k in range(2, dp):
        each(k, act_arrival)
        each(k, cot_arrival)
        each(k - 1, accumulate)
    each(dp - 1, accumulate)

    for h in range(2):
        both[s, :, pl.ds(h * half, half)] = grad[h].astype(BF16)
    swap = remote(both.at[s], both.at[s], swap_send, swap_recv, {"sub": 1 - s})
    swap.start()
    remote(both.at[1 - s], both.at[1 - s], swap_send, swap_recv, {"sub": 1 - s}).wait_recv()

    nt = (((1,), (1,)), ((), ()))
    whole = both[...].reshape(B, B)
    stat = lax.dot_general(whole, whole, nt, preferred_element_type=F32)
    mine = both[:, :, pl.ds(pl.multiple_of(s * half, half), half)].reshape(B, half)
    diagonal = lax.broadcasted_iota(jnp.int32, (B, B), 0) == lax.broadcasted_iota(jnp.int32, (B, B), 1)

    def total_of(x):
        return jnp.sum(jnp.sum(x, axis=0, keepdims=True), axis=1, keepdims=True)

    trace = total_of(jnp.where(diagonal, stat, 0.0))
    shift = DAMPING / B * trace
    damped = stat + jnp.where(diagonal, shift, 0.0)
    z_scale = 2.5 / jnp.sqrt(total_of(damped * damped))
    x = z_scale * damped
    xb = x.astype(BF16)
    x2 = jnp.dot(xb, xb, preferred_element_type=F32)
    d2 = 0.0625 * (10.0 * x - x2)
    fx = 0.25 * (5.0 * x - x2)
    d2b = d2.astype(BF16)
    d4 = 3.125 * d2 - jnp.dot(d2b, d2b, preferred_element_type=F32)
    w = jnp.dot(d4.astype(BF16), fx.astype(BF16), preferred_element_type=F32)
    kmat[...] = (0.3125 * x + 0.6103515625 * fx - 0.25 * w).astype(BF16)
    carried[...] = 1.5625 * mine.astype(F32) - jnp.dot(kmat[...], mine, preferred_element_type=F32)
    carried_b = carried[...].astype(BF16)
    gain = math.sqrt(B) * jnp.sqrt(z_scale)

    def deliver(k):
        there = lax.rem(z + k, dp)
        return remote(
            update.at[there], landed.at[z], out_send.at[k - 1], out_recv.at[k - 1], {"dp": there}
        )

    def delivered(k):
        came = lax.rem(z + dp - k, dp)
        return remote(
            update.at[came], landed.at[came], out_send.at[k - 1], out_recv.at[k - 1], {"dp": came}
        )

    def update_rows(there):
        at = pl.ds(pl.multiple_of(there * out_rows, out_rows), out_rows)
        product = jnp.dot(kmat[at, :], carried_b, preferred_element_type=F32)
        return (gain * (1.5625 * carried[at, :] - product)).astype(BF16)

    for k in sorted(range(1, dp), key=lambda k: min(k, dp - k)):
        there = lax.rem(z + k, dp)
        update[there] = update_rows(there)
        deliver(k).start()
    landed[z] = update_rows(z)

    def sent(side, d):
        send_act(d).wait_send()
        to_pair(cot.at[d, s, block_col], d).wait_send()
        for k in range(1, mp):
            share(d, k).wait_send()

        @pl.when(has_next[side])
        def _():
            for q in range(PIECES):
                pass_on(side, cot.at[d, s], d, q).wait_send()

    swap.wait_send()
    to_pair(cot_hbm.at[block_col], z).wait_send()
    for side in range(2):
        @pl.when(has_next[side])
        def _():
            for q in range(PIECES):
                pass_on(side, cot_hbm, z, q).wait_send()
    for k in range(1, dp):
        each(k, sent)
    for k in range(1, dp):
        deliver(k).wait_send()
        delivered(k).wait_recv()
    for slot in range(dp):
        out[slot] = landed[table[0, slot]]


def shards(dp, mp, activations, cotangent, owner_table):
    tokens = activations.shape[0]
    col_count, half = cotangent.shape[1:]
    cot = cotangent.transpose(1, 0, 2)
    hbm = pl.BlockSpec(memory_space=pltpu.HBM)
    dma = pltpu.SemaphoreType.DMA
    return pl.pallas_call(
        functools.partial(kernel, dp, mp, col_count),
        out_shape=jax.ShapeDtypeStruct((dp, B // dp, half), BF16),
        in_specs=[pl.BlockSpec(memory_space=pltpu.SMEM), hbm, hbm],
        out_specs=pl.BlockSpec(memory_space=pltpu.VMEM),
        scratch_shapes=[
            pltpu.VMEM((tokens, half), BF16),
            pltpu.VMEM((dp, 2, col_count, tokens, half), BF16),
            pltpu.VMEM((dp, mp, tokens // mp, half), BF16),
            pltpu.VMEM((2, half, B), BF16),
            pltpu.VMEM((2, half, half), F32),
            pltpu.VMEM((B, B), BF16),
            pltpu.VMEM((B, half), F32),
            pltpu.VMEM((dp, B // dp, half), BF16),
            pltpu.VMEM((dp, B // dp, half), BF16),
            dma((2,)), dma((dp,)), dma((dp,)), dma((dp, mp - 1)), dma((dp, mp - 1)), dma((2, dp, PIECES)), dma((dp, PIECES)),
            dma((dp,)), dma((dp,)), dma, dma, dma((dp - 1,)), dma((dp - 1,)),
        ],
        compiler_params=pltpu.CompilerParams(
            collective_id=0, has_side_effects=True, vmem_limit_bytes=60 * 1024 * 1024
        ),
    )(owner_table, activations, cot)


def solution(mesh):
    in_specs = (P(("rep", "dp"), None), P(("rep", "dp"), "mp", "sub"), P(("rep", "mp"), None))
    out_specs = P(("rep", "mp"), "dp", "sub")
    return jax.shard_map(
        functools.partial(shards, mesh.shape["dp"], mesh.shape["mp"]),
        mesh=mesh, in_specs=in_specs, out_specs=out_specs, check_vma=False,
    )
```
